32 devices in a mesh: rad: 8 (over z, x), az: 4 (over y, core).
Axes of the slice: x: 2, y: 2, z: 4, core: 2. Of those that a mesh axis runs over, the one named last changes fastest.
Arguments:
- state: float32 [6, 2, 256, 4096], P(None, None, 'rad', 'az'), may hold values from -4 to 4, as said below
- offsets: int32 [256], P('rad'), may hold values from 0 to 4095
- viscosity: float32 [2, 256, 4096], P(None, 'rad', 'az'), may hold values from 0.02 to 0.2
- absorb: float32 [2, 256, 4096], P(None, 'rad', 'az'), may hold values from 0.5 to 8
Outputs:
- new_state: float32 [6, 2, 256, 4096], P(None, None, 'rad', 'az')
- depth: float32 [2, 256, 4096], P(None, 'rad', 'az')
The draws below stay inside these ranges and needn't reach their ends.
Inputs may be any that keep to these rules, and one draw needn't show every extreme that they name: state[0] lies in 0.5 to 2, state[1], state[2], state[3] in -4 to 4, state[4] in 1 to 3, state[5] in 0.1 to 1.
All inputs are finite; a program needn't handle non-finite values.
Results may differ from the reference program's by a relative error of at most 0.00002.
Values sent between devices are 32-bit elements; how exact they have to be, the bound alone decides.
A program may use at most 128 MiB of HBM per device.

```python
import math
import jax
import jax.numpy as jnp
from jax import lax

P_SIZE = 2
NR = 256
NA = 4096


def draw_state(key, part):
    keys = jax.random.split(jax.random.fold_in(key, 11), 4)
    shape = (P_SIZE, NR, NA)
    density = jax.random.uniform(keys[0], shape, jnp.float32, 0.5, 2.0)
    energy = jax.random.uniform(keys[2], shape, jnp.float32, 1.0, 3.0)
    momenta = jnp.clip(jax.random.normal(keys[1], (3,) + shape, jnp.float32), -4.0, 4.0)
    dust = jnp.exp(jax.random.uniform(keys[3], shape, jnp.float32, math.log(0.1), 0.0))
    return jnp.concatenate([density[None], momenta, energy[None], dust[None]], axis=0)


def set_ends(result, rng, least, high):
    spot = [jax.random.randint(jax.random.fold_in(rng, axis), (), 0, length) for axis, length in enumerate(result.shape)]
    widest = result.shape.index(max(result.shape))
    next_to = spot[:widest] + [(spot[widest] + 1) % result.shape[widest]] + spot[widest + 1:]
    return result.at[tuple(spot)].set(least).at[tuple(next_to)].set(high)


def levels(rng, extent, cuts, low, top_value):
    def one(position, shards_of):
        heights = jax.random.uniform(jax.random.fold_in(jax.random.fold_in(rng, 6), position), (shards_of,), jnp.float32, low / len(cuts), top_value / len(cuts))
        return jnp.repeat(jnp.exp(heights), extent[position] // shards_of).reshape((-1,) + (1,) * (len(extent) - position - 1))

    factor_of = one(*cuts[0])
    for cut in cuts[1:]:
        factor_of = factor_of * one(*cut)
    return factor_of


def setup_inputs(seed: int = 0) -> dict:
    key_of = jax.random.split(jax.random.key(seed), 5)
    state = draw_state(jax.random.fold_in(key_of[4], 71), 0)
    offsets = set_ends(jax.random.randint(key_of[1], (NR,), 0, NA), jax.random.fold_in(key_of[1], 1), 0, NA - 1).astype(jnp.int32)
    viscosity = jnp.clip(jnp.exp(math.log(0.2) - 2.3025851 * jax.random.uniform(key_of[2], (P_SIZE, NR, NA), jnp.float32) ** levels(key_of[2], (P_SIZE, NR, NA), ((1, 8), (2, 4)), -0.2, 0.2)), 0.02, 0.2)
    absorb = jnp.clip(jnp.exp(math.log(8.0) - 2.7725887 * jax.random.uniform(key_of[3], (P_SIZE, NR, NA), jnp.float32) ** levels(key_of[3], (P_SIZE, NR, NA), ((1, 8), (2, 4)), -0.2, 0.2)), 0.5, 8.0)
    return {"state": state, "offsets": offsets, "viscosity": viscosity, "absorb": absorb}


AZIMUTH_COEF = 0.1


def roll_annulus(pair):
    return jnp.roll(pair[0], pair[1], axis=-1)


def reference(state, offsets, viscosity, absorb):
    annuli = jnp.moveaxis(state, 2, 0)
    shifted = lax.map(roll_annulus, (annuli, offsets))
    shifted = jnp.moveaxis(shifted, 0, 2)
    radial_pad = jnp.pad(shifted, ((0, 0), (0, 0), (1, 1), (0, 0)))
    radial_term = radial_pad[:, :, 2:] + radial_pad[:, :, :-2] - 2.0 * shifted
    azimuth_term = jnp.roll(shifted, 1, axis=3) + jnp.roll(shifted, -1, axis=3) - 2.0 * shifted
    smoothed = shifted + viscosity[None] * radial_term + AZIMUTH_COEF * azimuth_term
    depth_step = 2.0 * absorb * smoothed[5] / NR
    depth = jnp.cumsum(depth_step, axis=1) - 0.5 * depth_step
    radius = jnp.arange(NR).astype(jnp.float32) + 0.5
    stellar_flux = 1.0 / (1.0 + radius / NR)
    energy = smoothed[4] + stellar_flux[None, :, None] * jnp.exp(-depth)
    new_state = jnp.concatenate([smoothed[:4], energy[None], smoothed[5:]], axis=0)
    return new_state, depth
```

```python
import functools

import jax
import jax.numpy as jnp
from jax import lax
from jax.experimental import pallas as pl
from jax.experimental.pallas import tpu as pltpu
from jax.sharding import PartitionSpec as P

AZIMUTH_COEF = 0.1
LANES = 128
SUB = 8


def kernel(n_rad, n_az, state, offs, visc, absorb, out, depth, buf, sh, eo, ei, tot_out, tot_in, ss, rs):
    groups = n_az // 2
    rad = lax.axis_index("rad")
    az = lax.axis_index("az")
    core = lax.rem(az, 2)
    sibling = {"az": az + 1 - 2 * core}
    planes, rows, width = state.shape
    cols = width // LANES
    tiles = rows // SUB
    dust = planes - 2
    rest = dust
    total_rows = rows * n_rad

    def rad_at(k):
        return {"rad": lax.rem(rad + k + n_rad, n_rad)}

    def az_at(k):
        return {"az": lax.rem(az + 2 * k, n_az)}

    count = [0]

    def remote(src, dst, device):
        i = count[0]
        count[0] += 1
        return pltpu.make_async_remote_copy(
            src_ref=src, dst_ref=dst, send_sem=ss.at[i], recv_sem=rs.at[i],
            device_id=device, device_id_type=pl.DeviceIdType.MESH,
        )

    peers = [az_at(k) for k in range(1, groups)] + [sibling] + [rad_at(k) for k in range(1, n_rad)]
    barrier = pltpu.get_barrier_semaphore()
    for peer in peers:
        pl.semaphore_signal(barrier, inc=1, device_id=peer, device_id_type=pl.DeviceIdType.MESH)
    pl.semaphore_wait(barrier, len(peers))

    pieces = [(dust, 2, 0, rows)]
    edge_tiles = [0, tiles - 1]
    for t in edge_tiles + list(range(1, tiles - 2)):
        pieces.append((0, rest, t * SUB, SUB))
    half = rest // 2
    pieces.append((0, half, (tiles - 2) * SUB, SUB))
    pieces.append((half, rest - half, (tiles - 2) * SUB, SUB))

    sent = []
    across, beside = [], []
    for p0, np_, r0, nr in pieces:
        ps, rws = pl.ds(p0, np_), pl.ds(r0, nr)
        across.append([remote(state.at[ps, rws], buf.at[2 * k - 1, ps, rws], az_at(k)) for k in range(1, groups)])
        beside.append(remote(state.at[ps, rws], buf.at[0, ps, rws], sibling))
        for c in across[-1] + [beside[-1]]:
            c.start()
            sent.append(c)

    def arrive(i):
        p0, np_, r0, nr = pieces[i]
        ps, rws = pl.ds(p0, np_), pl.ds(r0, nr)
        forwards = []
        for k in range(1, groups):
            across[i][k - 1].wait_recv()
            f = remote(buf.at[2 * k - 1, ps, rws], buf.at[2 * k, ps, rws], sibling)
            f.start()
            sent.append(f)
            forwards.append(f)
        beside[i].wait_recv()
        for f in forwards:
            f.wait_recv()

    lane = lax.broadcasted_iota(jnp.int32, (SUB, LANES), 1)

    def shift_tile(tile, p0, np_):
        r = pl.ds(tile * SUB, SUB)
        amount = offs[r, :]
        block = amount // width
        within = amount - block * width
        column = within // LANES
        rem = within - column * LANES
        pick = (lane - rem) & (LANES - 1)
        low = lane < rem

        def one(p, carry):
            def load(d, c):
                cs = pl.ds(c * LANES, LANES)
                if d == 0:
                    return state[p, r, cs]
                if d % 2 == 0:
                    return buf[d - 1, p, r, cs]
                slot = jnp.where(core == 1, d, (d + 2) % n_az)
                return buf[slot - 1, p, r, cs]

            line = []
            for move, c in [(1, c) for c in range(cols)] + [(0, c) for c in range(cols)] + [(-1, 0)]:
                value = load(move % n_az, c)
                for b in range(1, n_az):
                    value = jnp.where(block == b, load((b + move) % n_az, c), value)
                line.append(value)
            step = cols // 2
            while step:
                chosen = (column & step) != 0
                line = [jnp.where(chosen, line[i - step], line[i]) for i in range(step, len(line))]
                step //= 2
            turned = [jnp.take_along_axis(v, pick, axis=1, mode="promise_in_bounds") for v in line]
            x = [turned[0]] + [jnp.where(low, turned[j - 1], turned[j]) for j in range(1, len(turned))]
            right = [pltpu.roll(v, 1, 1) for v in x[:-1]]
            left = [pltpu.roll(v, LANES - 1, 1) for v in x[1:]]
            for c in range(cols):
                cs = pl.ds(c * LANES, LANES)
                mid = x[c + 1]
                prev = jnp.where(lane == 0, right[c], right[c + 1])
                nxt = jnp.where(lane == LANES - 1, left[c + 1], left[c])
                sh[p, pl.ds(SUB + tile * SUB, SUB), cs] = mid
                out[p, r, cs] = mid + AZIMUTH_COEF * (nxt + prev - 2.0 * mid)
                if tile == 0:
                    eo[0, p, :, cs] = mid[:1]
                if tile == tiles - 1:
                    eo[1, p, :, cs] = mid[SUB - 1:]
            return carry

        lax.fori_loop(p0, p0 + np_, one, 0)

    def send_edge(side, p0, np_):
        ps = pl.ds(p0, np_)
        c = remote(eo.at[side, ps], ei.at[1 - side, ps], rad_at(-1 if side == 0 else 1))
        c.start()
        sent.append(c)
        return c

    def place_edges(p0, np_):
        def one(p, carry):
            sh[p, SUB - 1:SUB, :] = jnp.where(rad > 0, ei[0, p], 0.0)
            sh[p, SUB + rows:SUB + rows + 1, :] = jnp.where(rad < n_rad - 1, ei[1, p], 0.0)
            return carry

        lax.fori_loop(p0, p0 + np_, one, 0)

    def smooth(tile, p0, np_):
        top = SUB + tile * SUB

        def one(p, carry):
            r = pl.ds(tile * SUB, SUB)
            mid = sh[p, top:top + SUB, :]
            up = sh[p, top - 1:top + SUB - 1, :]
            down = sh[p, top + 1:top + SUB + 1, :]
            out[p, r, :] = out[p, r, :] + visc[lax.rem(p, 2), r, :] * (down + up - 2.0 * mid)
            return carry

        lax.fori_loop(p0, p0 + np_, one, 0)

    arrive(0)
    for t in range(tiles):
        shift_tile(t, dust, 2)
    edges = [send_edge(s, dust, 2) for s in (0, 1)]
    for e in edges:
        e.wait_recv()
    place_edges(dust, 2)
    for t in range(tiles):
        smooth(t, dust, 2)

    row = lax.broadcasted_iota(jnp.int32, (SUB, width), 0)
    for h in range(2):
        base = jnp.zeros((1, width), jnp.float32)
        for t in range(tiles):
            r = pl.ds(t * SUB, SUB)
            step = 2.0 * absorb[h, r, :] * out[dust + h, r, :] / total_rows
            run = step
            for k in (1, 2, 4):
                run = run + jnp.where(row >= k, pltpu.roll(run, k, 0), 0.0)
            run = run + base
            depth[h, r, :] = run - 0.5 * step
            base = run[SUB - 1:]
        tot_out[h] = base
    totals = []
    for k in range(1, n_rad):
        c = remote(tot_out, tot_in.at[k - 1], rad_at(k))
        c.start()
        sent.append(c)
        totals.append(c)

    arrive(1)
    shift_tile(0, 0, rest)
    edge_in = send_edge(0, 0, rest)
    arrive(2)
    shift_tile(tiles - 1, 0, rest)
    edge_out = send_edge(1, 0, rest)

    for c in totals:
        c.wait_recv()
    for h in range(2):
        carried = jnp.zeros((1, width), jnp.float32)
        for k in range(1, n_rad):
            carried = carried + jnp.where(k <= rad, tot_in[k - 1, h], 0.0)
        for t in range(tiles):
            r = pl.ds(t * SUB, SUB)
            depth[h, r, :] = depth[h, r, :] + carried

    edge_in.wait_recv()
    edge_out.wait_recv()
    place_edges(0, rest)
    i = 3
    for t in range(1, tiles - 2):
        arrive(i)
        shift_tile(t, 0, rest)
        smooth(t - 1, 0, rest)
        i += 1

    def last(p0, np_):
        shift_tile(tiles - 2, p0, np_)
        for t in range(max(tiles - 3, 0), tiles):
            smooth(t, p0, np_)

    arrive(i)
    last(0, half)
    arrive(i + 1)
    last(half, rest - half)
    for h in range(2):
        for t in range(tiles):
            r = pl.ds(t * SUB, SUB)
            radius = (rad * rows + t * SUB + row).astype(jnp.float32) + 0.5
            flux = 1.0 / (1.0 + radius / total_rows)
            out[rest - 2 + h, r, :] = out[rest - 2 + h, r, :] + flux * jnp.exp(-depth[h, r, :])
    for c in sent:
        c.wait_send()


def body(n_rad, n_az, state, offsets, viscosity, absorb):
    fields, polar, rows, width = state.shape
    planes = fields * polar
    groups = n_az // 2
    tiles = rows // SUB
    n_pieces = 1 + 2 + max(tiles - 3, 0) + 2
    n_sems = n_pieces * (2 * (groups - 1) + 1) + 4 + n_rad - 1
    offs = jnp.broadcast_to(offsets[:, None], (rows, LANES))
    f32 = jnp.float32
    vm = pl.BlockSpec(memory_space=pltpu.VMEM)
    new_state, depth = pl.pallas_call(
        functools.partial(kernel, n_rad, n_az),
        out_shape=(
            jax.ShapeDtypeStruct((planes, rows, width), f32),
            jax.ShapeDtypeStruct((polar, rows, width), f32),
        ),
        in_specs=[vm] * 4,
        out_specs=(vm, vm),
        scratch_shapes=[
            pltpu.VMEM((n_az - 1, planes, rows, width), f32),
            pltpu.VMEM((planes, rows + 2 * SUB, width), f32),
            pltpu.VMEM((2, planes, 1, width), f32),
            pltpu.VMEM((2, planes, 1, width), f32),
            pltpu.VMEM((polar, 1, width), f32),
            pltpu.VMEM((n_rad - 1, polar, 1, width), f32),
            pltpu.SemaphoreType.DMA((n_sems,)),
            pltpu.SemaphoreType.DMA((n_sems,)),
        ],
        compiler_params=pltpu.CompilerParams(
            collective_id=0, has_side_effects=True, vmem_limit_bytes=56 * 2**20
        ),
    )(state.reshape(planes, rows, width), offs, viscosity, absorb)
    return new_state.reshape(state.shape), depth


def solution(mesh):
    in_specs = (P(None, None, "rad", "az"), P("rad"), P(None, "rad", "az"), P(None, "rad", "az"))
    out_specs = (P(None, None, "rad", "az"), P(None, "rad", "az"))
    f = functools.partial(body, mesh.shape["rad"], mesh.shape["az"])
    return jax.shard_map(f, mesh=mesh, in_specs=in_specs, out_specs=out_specs, check_vma=False)
```

```python
import functools

import jax
import jax.numpy as jnp
from jax import lax
from jax.experimental import pallas as pl
from jax.experimental.pallas import tpu as pltpu
from jax.sharding import PartitionSpec as P

AZIMUTH_COEF = 0.1
LANES = 128
SUB = 8


def tail_planes(rest):
    cuts = [0, rest * 4 // 10, rest * 7 // 10, rest * 9 // 10, rest]
    return [(a, b - a) for a, b in zip(cuts, cuts[1:]) if b > a]


def kernel(n_rad, n_az, source, offs, visc, absorb, result, depth, carry_out, heat,
           state, out, buf, sh, eo, ei, tot_out, tot_in, ss, rs, ls):
    groups = n_az // 2
    rad = lax.axis_index("rad")
    az = lax.axis_index("az")
    core = lax.rem(az, 2)
    sibling = {"az": az + 1 - 2 * core}
    planes, rows, width = state.shape
    cols = width // LANES
    tiles = rows // SUB
    dust = planes - 2
    rest = dust
    total_rows = rows * n_rad

    def rad_at(k):
        return {"rad": lax.rem(rad + k + n_rad, n_rad)}

    def az_at(k):
        return {"az": lax.rem(az + 2 * k, n_az)}

    count = [0]

    def remote(src, dst, device):
        i = count[0]
        count[0] += 1
        return pltpu.make_async_remote_copy(
            src_ref=src, dst_ref=dst, send_sem=ss.at[i], recv_sem=rs.at[i],
            device_id=device, device_id_type=pl.DeviceIdType.MESH,
        )

    fetch = pltpu.make_async_copy(source, state, ls.at[0])
    fetch.start()
    stored = []

    def store(p0, np_, r0, nr):
        at = (pl.ds(p0, np_), pl.ds(r0, nr))
        c = pltpu.make_async_copy(out.at[at], result.at[at], ls.at[1 + len(stored)])
        c.start()
        stored.append(c)

    peers = [az_at(k) for k in range(1, groups)] + [sibling] + [rad_at(k) for k in range(1, n_rad)]
    barrier = pltpu.get_barrier_semaphore()
    for peer in peers:
        pl.semaphore_signal(barrier, inc=1, device_id=peer, device_id_type=pl.DeviceIdType.MESH)
    pl.semaphore_wait(barrier, len(peers))

    pieces = [(dust, 2, 0, rows)]
    edge_tiles = [0, tiles - 1]
    for t in edge_tiles + list(range(1, tiles - 2)):
        pieces.append((0, rest, t * SUB, SUB))
    tail = tail_planes(rest)
    for p0, np_ in tail:
        pieces.append((p0, np_, (tiles - 2) * SUB, SUB))

    sent = []
    across, beside = [], []
    for p0, np_, r0, nr in pieces:
        ps, rws = pl.ds(p0, np_), pl.ds(r0, nr)
        across.append([remote(source.at[ps, rws], buf.at[2 * k - 1, ps, rws], az_at(k)) for k in range(1, groups)])
        beside.append(remote(source.at[ps, rws], buf.at[0, ps, rws], sibling))
        for c in across[-1] + [beside[-1]]:
            c.start()
            sent.append(c)

    def arrive(i):
        p0, np_, r0, nr = pieces[i]
        ps, rws = pl.ds(p0, np_), pl.ds(r0, nr)
        forwards = []
        for k in range(1, groups):
            across[i][k - 1].wait_recv()
            f = remote(buf.at[2 * k - 1, ps, rws], buf.at[2 * k, ps, rws], sibling)
            f.start()
            sent.append(f)
            forwards.append(f)
        beside[i].wait_recv()
        for f in forwards:
            f.wait_recv()

    lane = lax.broadcasted_iota(jnp.int32, (SUB, LANES), 1)

    def shift_tile(tile, p0, np_):
        r = pl.ds(tile * SUB, SUB)
        sub = lax.broadcasted_iota(jnp.int32, (SUB, LANES), 0)
        amount = jnp.full((SUB, LANES), offs[tile * SUB], jnp.int32)
        for k in range(1, SUB):
            amount = jnp.where(sub == k, offs[tile * SUB + k], amount)
        block = amount // width
        within = amount - block * width
        column = within // LANES
        rem = within - column * LANES
        pick = (lane - rem) & (LANES - 1)
        low = lane < rem

        def one(p, carry):
            def load(d, c):
                cs = pl.ds(c * LANES, LANES)
                if d == 0:
                    return state[p, r, cs]
                if d % 2 == 0:
                    return buf[d - 1, p, r, cs]
                slot = jnp.where(core == 1, d, (d + 2) % n_az)
                return buf[slot - 1, p, r, cs]

            line = []
            for move, c in [(1, c) for c in range(cols)] + [(0, c) for c in range(cols)] + [(-1, 0)]:
                value = load(move % n_az, c)
                for b in range(1, n_az):
                    value = jnp.where(block == b, load((b + move) % n_az, c), value)
                line.append(value)
            step = cols // 2
            while step:
                chosen = (column & step) != 0
                line = [jnp.where(chosen, line[i - step], line[i]) for i in range(step, len(line))]
                step //= 2
            turned = [jnp.take_along_axis(v, pick, axis=1, mode="promise_in_bounds") for v in line]
            x = [turned[0]] + [jnp.where(low, turned[j - 1], turned[j]) for j in range(1, len(turned))]
            right = [pltpu.roll(v, 1, 1) for v in x[:-1]]
            left = [pltpu.roll(v, LANES - 1, 1) for v in x[1:]]
            for c in range(cols):
                cs = pl.ds(c * LANES, LANES)
                mid = x[c + 1]
                prev = jnp.where(lane == 0, right[c], right[c + 1])
                nxt = jnp.where(lane == LANES - 1, left[c + 1], left[c])
                sh[p, pl.ds(SUB + tile * SUB, SUB), cs] = mid
                out[p, r, cs] = mid + AZIMUTH_COEF * (nxt + prev - 2.0 * mid)
                if tile == 0:
                    eo[0, p, :, cs] = mid[:1]
                if tile == tiles - 1:
                    eo[1, p, :, cs] = mid[SUB - 1:]
            return carry

        lax.fori_loop(p0, p0 + np_, one, 0)

    def send_edge(side, p0, np_):
        ps = pl.ds(p0, np_)
        c = remote(eo.at[side, ps], ei.at[1 - side, ps], rad_at(-1 if side == 0 else 1))
        c.start()
        sent.append(c)
        return c

    def place_edges(p0, np_):
        def one(p, carry):
            sh[p, SUB - 1:SUB, :] = jnp.where(rad > 0, ei[0, p], 0.0)
            sh[p, SUB + rows:SUB + rows + 1, :] = jnp.where(rad < n_rad - 1, ei[1, p], 0.0)
            return carry

        lax.fori_loop(p0, p0 + np_, one, 0)

    def smooth(tile, p0, np_):
        top = SUB + tile * SUB

        def one(p, carry):
            r = pl.ds(tile * SUB, SUB)
            mid = sh[p, top:top + SUB, :]
            up = sh[p, top - 1:top + SUB - 1, :]
            down = sh[p, top + 1:top + SUB + 1, :]
            out[p, r, :] = out[p, r, :] + visc[lax.rem(p, 2), r, :] * (down + up - 2.0 * mid)
            return carry

        lax.fori_loop(p0, p0 + np_, one, 0)

    arrive(0)
    fetch.wait()
    for t in range(tiles):
        shift_tile(t, dust, 2)
    edges = [send_edge(s, dust, 2) for s in (0, 1)]
    for e in edges:
        e.wait_recv()
    place_edges(dust, 2)
    for t in range(tiles):
        smooth(t, dust, 2)
    store(dust, 2, 0, rows)

    row = lax.broadcasted_iota(jnp.int32, (SUB, width), 0)
    for h in range(2):
        base = jnp.zeros((1, width), jnp.float32)
        for t in range(tiles):
            r = pl.ds(t * SUB, SUB)
            step = 2.0 * absorb[h, r, :] * out[dust + h, r, :] / total_rows
            run = step
            for k in (1, 2, 4):
                run = run + jnp.where(row >= k, pltpu.roll(run, k, 0), 0.0)
            run = run + base
            depth[h, r, :] = run - 0.5 * step
            base = run[SUB - 1:]
        tot_out[h] = base
    totals = []
    for k in range(1, n_rad):
        c = remote(tot_out, tot_in.at[k - 1], rad_at(k))
        c.start()
        sent.append(c)
        totals.append(c)

    arrive(1)
    shift_tile(0, 0, rest)
    edge_in = send_edge(0, 0, rest)
    arrive(2)
    shift_tile(tiles - 1, 0, rest)
    edge_out = send_edge(1, 0, rest)

    for c in totals:
        c.wait_recv()
    for h in range(2):
        carried = jnp.zeros((1, width), jnp.float32)
        for k in range(1, n_rad):
            carried = carried + jnp.where(k <= rad, tot_in[k - 1, h], 0.0)
        carry_out[h:h + 1, :] = carried
        for t in range(tiles):
            r = pl.ds(t * SUB, SUB)
            radius = (rad * rows + t * SUB + row).astype(jnp.float32) + 0.5
            flux = 1.0 / (1.0 + radius / total_rows)
            heat[h, r, :] = flux * jnp.exp(-(depth[h, r, :] + carried))

    edge_in.wait_recv()
    edge_out.wait_recv()
    place_edges(0, rest)
    i = 3
    for t in range(1, tiles - 2):
        arrive(i)
        shift_tile(t, 0, rest)
        smooth(t - 1, 0, rest)
        store(0, rest, (t - 1) * SUB, SUB)
        i += 1
    first = max(tiles - 3, 0)
    for p0, np_ in tail:
        arrive(i)
        shift_tile(tiles - 2, p0, np_)
        for t in range(first, tiles):
            smooth(t, p0, np_)
        store(p0, np_, first * SUB, (tiles - first) * SUB)
        i += 1
    for c in stored:
        c.wait()
    for c in sent:
        c.wait_send()


def body(n_rad, n_az, state, offsets, viscosity, absorb):
    fields, polar, rows, width = state.shape
    planes = fields * polar
    groups = n_az // 2
    tiles = rows // SUB
    n_tail = len(tail_planes(planes - 2))
    n_pieces = 1 + 2 + max(tiles - 3, 0) + n_tail
    n_sems = n_pieces * (2 * (groups - 1) + 1) + 4 + n_rad - 1
    f32 = jnp.float32
    vm = pl.BlockSpec(memory_space=pltpu.VMEM)
    hbm = pl.BlockSpec(memory_space=pl.ANY)
    moved, local, carried, heat = pl.pallas_call(
        functools.partial(kernel, n_rad, n_az),
        out_shape=(
            jax.ShapeDtypeStruct((planes, rows, width), f32),
            jax.ShapeDtypeStruct((polar, rows, width), f32),
            jax.ShapeDtypeStruct((polar, width), f32),
            jax.ShapeDtypeStruct((polar, rows, width), f32),
        ),
        in_specs=[hbm, pl.BlockSpec(memory_space=pltpu.SMEM), vm, vm],
        out_specs=(hbm, vm, vm, vm),
        scratch_shapes=[
            pltpu.VMEM((planes, rows, width), f32),
            pltpu.VMEM((planes, rows, width), f32),
            pltpu.VMEM((n_az - 1, planes, rows, width), f32),
            pltpu.VMEM((planes, rows + 2 * SUB, width), f32),
            pltpu.VMEM((2, planes, 1, width), f32),
            pltpu.VMEM((2, planes, 1, width), f32),
            pltpu.VMEM((polar, 1, width), f32),
            pltpu.VMEM((n_rad - 1, polar, 1, width), f32),
            pltpu.SemaphoreType.DMA((n_sems,)),
            pltpu.SemaphoreType.DMA((n_sems,)),
            pltpu.SemaphoreType.DMA((2 + max(tiles - 3, 0) + n_tail,)),
        ],
        compiler_params=pltpu.CompilerParams(
            collective_id=0, has_side_effects=True, vmem_limit_bytes=56 * 2**20
        ),
    )(state.reshape(planes, rows, width), offsets, viscosity, absorb)
    moved = moved.reshape(state.shape)
    field = lax.broadcasted_iota(jnp.int32, state.shape, 0)
    return jnp.where(field == fields - 2, moved + heat[None], moved), local + carried[:, None, :]


def solution(mesh):
    in_specs = (P(None, None, "rad", "az"), P("rad"), P(None, "rad", "az"), P(None, "rad", "az"))
    out_specs = (P(None, None, "rad", "az"), P(None, "rad", "az"))
    f = functools.partial(body, mesh.shape["rad"], mesh.shape["az"])
    return jax.shard_map(f, mesh=mesh, in_specs=in_specs, out_specs=out_specs, check_vma=False)
```

```python
import functools

import jax
import jax.numpy as jnp
from jax import lax
from jax.experimental import pallas as pl
from jax.experimental.pallas import tpu as pltpu
from jax.sharding import PartitionSpec as P

AZIMUTH_COEF = 0.1
LANES = 128
SUB = 8


def tail_planes(rest):
    cuts = [0, rest // 2, rest]
    return [(a, b - a) for a, b in zip(cuts, cuts[1:]) if b > a]


def kernel(n_rad, n_az, source, offs, visc, absorb, result, depth,
           heat, state, out, buf, sh, eo, ei, tot_out, tot_in, ss, rs, ls):
    groups = n_az // 2
    rad = lax.axis_index("rad")
    az = lax.axis_index("az")
    core = lax.rem(az, 2)
    sibling = {"az": az + 1 - 2 * core}
    planes, rows, width = state.shape
    cols = width // LANES
    tiles = rows // SUB
    dust = planes - 2
    rest = dust
    total_rows = rows * n_rad

    def rad_at(k):
        return {"rad": lax.rem(rad + k + n_rad, n_rad)}

    def az_at(k):
        return {"az": lax.rem(az + 2 * k, n_az)}

    count = [0]

    def remote(src, dst, device):
        i = count[0]
        count[0] += 1
        return pltpu.make_async_remote_copy(
            src_ref=src, dst_ref=dst, send_sem=ss.at[i], recv_sem=rs.at[i],
            device_id=device, device_id_type=pl.DeviceIdType.MESH,
        )

    fetch = pltpu.make_async_copy(source, state, ls.at[0])
    fetch.start()
    stored = []

    def store(p0, np_, r0, nr):
        at = (pl.ds(p0, np_), pl.ds(r0, nr))
        c = pltpu.make_async_copy(out.at[at], result.at[at], ls.at[1 + len(stored)])
        c.start()
        stored.append(c)

    inner, outer = rad > 0, rad < n_rad - 1
    ei[...] = jnp.zeros_like(ei)
    tot_in[...] = jnp.zeros_like(tot_in)
    peers = [az_at(k) for k in range(1, groups)] + [sibling]
    barrier = pltpu.get_barrier_semaphore()
    for there, k in ((inner, -1), (outer, 1)):
        @pl.when(there)
        def _():
            pl.semaphore_signal(barrier, inc=1, device_id=rad_at(k), device_id_type=pl.DeviceIdType.MESH)
    for peer in peers:
        pl.semaphore_signal(barrier, inc=1, device_id=peer, device_id_type=pl.DeviceIdType.MESH)
    senders = len(peers)
    d = 1
    while d < n_rad:
        if d > 1:
            @pl.when(rad >= d)
            def _():
                pl.semaphore_signal(barrier, inc=1, device_id=rad_at(-d), device_id_type=pl.DeviceIdType.MESH)
            senders = senders + (rad + d < n_rad).astype(jnp.int32)
        d *= 2
    pl.semaphore_wait(barrier, senders + inner.astype(jnp.int32) + outer.astype(jnp.int32))

    pieces = [(dust, 2, 0, rows)]
    edge_tiles = [0, tiles - 1]
    for t in edge_tiles + list(range(1, tiles - 2)):
        pieces.append((0, rest, t * SUB, SUB))
    tail = tail_planes(rest)
    for p0, np_ in tail:
        pieces.append((p0, np_, (tiles - 2) * SUB, SUB))

    sent, chained = [], []
    across, beside = [], []
    for p0, np_, r0, nr in pieces:
        ps, rws = pl.ds(p0, np_), pl.ds(r0, nr)
        across.append([remote(source.at[ps, rws], buf.at[2 * k - 1, ps, rws], az_at(k)) for k in range(1, groups)])
        beside.append(remote(source.at[ps, rws], buf.at[0, ps, rws], sibling))
        for c in across[-1] + [beside[-1]]:
            c.start()
            sent.append(c)

    def arrive(i):
        p0, np_, r0, nr = pieces[i]
        ps, rws = pl.ds(p0, np_), pl.ds(r0, nr)
        forwards = []
        for k in range(1, groups):
            across[i][k - 1].wait_recv()
            f = remote(buf.at[2 * k - 1, ps, rws], buf.at[2 * k, ps, rws], sibling)
            f.start()
            sent.append(f)
            forwards.append(f)
        beside[i].wait_recv()
        for f in forwards:
            f.wait_recv()

    lane = lax.broadcasted_iota(jnp.int32, (SUB, LANES), 1)

    def shift_tile(tile, p0, np_):
        r = pl.ds(tile * SUB, SUB)
        sub = lax.broadcasted_iota(jnp.int32, (SUB, LANES), 0)
        amount = jnp.full((SUB, LANES), offs[tile * SUB], jnp.int32)
        for k in range(1, SUB):
            amount = jnp.where(sub == k, offs[tile * SUB + k], amount)
        block = amount // width
        within = amount - block * width
        column = within // LANES
        rem = within - column * LANES
        pick = (lane - rem) & (LANES - 1)
        low = lane < rem

        def one(p, carry):
            def load(d, c):
                cs = pl.ds(c * LANES, LANES)
                if d == 0:
                    return state[p, r, cs]
                if d % 2 == 0:
                    return buf[d - 1, p, r, cs]
                slot = jnp.where(core == 1, d, (d + 2) % n_az)
                return buf[slot - 1, p, r, cs]

            line = []
            for move, c in [(1, c) for c in range(cols)] + [(0, c) for c in range(cols)] + [(-1, 0)]:
                value = load(move % n_az, c)
                for b in range(1, n_az):
                    value = jnp.where(block == b, load((b + move) % n_az, c), value)
                line.append(value)
            step = cols // 2
            while step:
                chosen = (column & step) != 0
                line = [jnp.where(chosen, line[i - step], line[i]) for i in range(step, len(line))]
                step //= 2
            turned = [jnp.take_along_axis(v, pick, axis=1, mode="promise_in_bounds") for v in line]
            x = [turned[0]] + [jnp.where(low, turned[j - 1], turned[j]) for j in range(1, len(turned))]
            right = [pltpu.roll(v, 1, 1) for v in x[:-1]]
            left = [pltpu.roll(v, LANES - 1, 1) for v in x[1:]]
            for c in range(cols):
                cs = pl.ds(c * LANES, LANES)
                mid = x[c + 1]
                prev = jnp.where(lane == 0, right[c], right[c + 1])
                nxt = jnp.where(lane == LANES - 1, left[c + 1], left[c])
                sh[p, pl.ds(SUB + tile * SUB, SUB), cs] = mid
                out[p, r, cs] = mid + AZIMUTH_COEF * (nxt + prev - 2.0 * mid)
                if tile == 0:
                    eo[0, p, :, cs] = mid[:1]
                if tile == tiles - 1:
                    eo[1, p, :, cs] = mid[SUB - 1:]
            return carry

        lax.fori_loop(p0, p0 + np_, one, 0)

    hops = []

    def scan_send():
        i = len(hops)
        d = 1 << i
        if d < n_rad:
            c = remote(tot_out.at[i], tot_in.at[i], rad_at(d))
            goes = rad + d < n_rad
            pl.when(goes)(c.start)
            chained.append((goes, c))
            hops.append(c)

    def scan_take():
        i = len(hops) - 1
        pl.when(rad >= 1 << i)(hops[i].wait_recv)
        tot_out[i + 1] = tot_out[i] + tot_in[i]

    def send_edge(side, p0, np_):
        ps = pl.ds(p0, np_)
        c = remote(eo.at[side, ps], ei.at[1 - side, ps], rad_at(-1 if side == 0 else 1))
        goes, comes = (inner, outer) if side == 0 else (outer, inner)
        pl.when(goes)(c.start)
        chained.append((goes, c))
        return comes, c

    def edge_wait(edge):
        pl.when(edge[0])(edge[1].wait_recv)

    def place_edges(p0, np_):
        def one(p, carry):
            sh[p, SUB - 1:SUB, :] = jnp.where(rad > 0, ei[0, p], 0.0)
            sh[p, SUB + rows:SUB + rows + 1, :] = jnp.where(rad < n_rad - 1, ei[1, p], 0.0)
            return carry

        lax.fori_loop(p0, p0 + np_, one, 0)

    def smooth(tile, p0, np_):
        top = SUB + tile * SUB

        def one(p, carry):
            r = pl.ds(tile * SUB, SUB)
            mid = sh[p, top:top + SUB, :]
            up = sh[p, top - 1:top + SUB - 1, :]
            down = sh[p, top + 1:top + SUB + 1, :]
            out[p, r, :] = out[p, r, :] + visc[lax.rem(p, 2), r, :] * (down + up - 2.0 * mid)
            return carry

        lax.fori_loop(p0, p0 + np_, one, 0)

    arrive(0)
    fetch.wait()
    for t in range(tiles):
        shift_tile(t, dust, 2)
    edges = [send_edge(s, dust, 2) for s in (0, 1)]
    for e in edges:
        edge_wait(e)
    place_edges(dust, 2)
    for t in range(tiles):
        smooth(t, dust, 2)
    store(dust, 2, 0, rows)

    row = lax.broadcasted_iota(jnp.int32, (SUB, width), 0)
    for h in range(2):
        base = jnp.zeros((1, width), jnp.float32)
        for t in range(tiles):
            r = pl.ds(t * SUB, SUB)
            step = 2.0 * absorb[h, r, :] * out[dust + h, r, :] / total_rows
            run = step
            for k in (1, 2, 4):
                run = run + jnp.where(row >= k, pltpu.roll(run, k, 0), 0.0)
            run = run + base
            depth[h, r, :] = run - 0.5 * step
            base = run[SUB - 1:]
        tot_out[0, h] = base
    scan_send()
    arrive(1)
    shift_tile(0, 0, rest)
    edge_in = send_edge(0, 0, rest)
    scan_take()
    scan_send()
    arrive(2)
    shift_tile(tiles - 1, 0, rest)
    edge_out = send_edge(1, 0, rest)

    scan_take()
    while 1 << len(hops) < n_rad:
        scan_send()
        scan_take()
    for h in range(2):
        carried = tot_in[0, h]
        for i in range(1, len(hops)):
            carried = carried + tot_in[i, h]
        for t in range(tiles):
            r = pl.ds(t * SUB, SUB)
            radius = (rad * rows + t * SUB + row).astype(jnp.float32) + 0.5
            flux = 1.0 / (1.0 + radius / total_rows)
            depth[h, r, :] = depth[h, r, :] + carried
            heat[h, r, :] = flux * jnp.exp(-depth[h, r, :])

    def warm(tile):
        r = pl.ds(tile * SUB, SUB)
        for h in range(2):
            out[rest - 2 + h, r, :] = out[rest - 2 + h, r, :] + heat[h, r, :]

    edge_wait(edge_in)
    edge_wait(edge_out)
    place_edges(0, rest)
    i = 3
    for t in range(1, tiles - 2):
        arrive(i)
        shift_tile(t, 0, rest)
        smooth(t - 1, 0, rest)
        warm(t - 1)
        store(0, rest, (t - 1) * SUB, SUB)
        i += 1
    first = max(tiles - 3, 0)
    for p0, np_ in tail:
        arrive(i)
        shift_tile(tiles - 2, p0, np_)
        for t in range(first, tiles):
            smooth(t, p0, np_)
            if p0 + np_ == rest:
                warm(t)
        store(p0, np_, first * SUB, (tiles - first) * SUB)
        i += 1
    for c in stored:
        c.wait()
    for goes, c in chained:
        pl.when(goes)(c.wait_send)
    for c in sent:
        c.wait_send()


def body(n_rad, n_az, state, offsets, viscosity, absorb):
    fields, polar, rows, width = state.shape
    planes = fields * polar
    groups = n_az // 2
    tiles = rows // SUB
    n_tail = len(tail_planes(planes - 2))
    n_pieces = 1 + 2 + max(tiles - 3, 0) + n_tail
    n_scan = (n_rad - 1).bit_length()
    n_sems = n_pieces * (2 * (groups - 1) + 1) + 4 + n_scan
    f32 = jnp.float32
    vm = pl.BlockSpec(memory_space=pltpu.VMEM)
    hbm = pl.BlockSpec(memory_space=pl.ANY)
    moved, local = pl.pallas_call(
        functools.partial(kernel, n_rad, n_az),
        out_shape=(
            jax.ShapeDtypeStruct((planes, rows, width), f32),
            jax.ShapeDtypeStruct((polar, rows, width), f32),
        ),
        in_specs=[hbm, pl.BlockSpec(memory_space=pltpu.SMEM), vm, vm],
        out_specs=(hbm, vm),
        scratch_shapes=[
            pltpu.VMEM((polar, rows, width), f32),
            pltpu.VMEM((planes, rows, width), f32),
            pltpu.VMEM((planes, rows, width), f32),
            pltpu.VMEM((n_az - 1, planes, rows, width), f32),
            pltpu.VMEM((planes, rows + 2 * SUB, width), f32),
            pltpu.VMEM((2, planes, 1, width), f32),
            pltpu.VMEM((2, planes, 1, width), f32),
            pltpu.VMEM((n_scan + 1, polar, 1, width), f32),
            pltpu.VMEM((n_scan, polar, 1, width), f32),
            pltpu.SemaphoreType.DMA((n_sems,)),
            pltpu.SemaphoreType.DMA((n_sems,)),
            pltpu.SemaphoreType.DMA((2 + max(tiles - 3, 0) + n_tail,)),
        ],
        compiler_params=pltpu.CompilerParams(
            collective_id=0, has_side_effects=True, vmem_limit_bytes=56 * 2**20
        ),
    )(state.reshape(planes, rows, width), offsets, viscosity, absorb)
    moved = moved.reshape(state.shape)
    return moved, local


def solution(mesh):
    in_specs = (P(None, None, "rad", "az"), P("rad"), P(None, "rad", "az"), P(None, "rad", "az"))
    out_specs = (P(None, None, "rad", "az"), P(None, "rad", "az"))
    f = functools.partial(body, mesh.shape["rad"], mesh.shape["az"])
    return jax.shard_map(f, mesh=mesh, in_specs=in_specs, out_specs=out_specs, check_vma=False)
```

```python
import functools

import jax
import jax.numpy as jnp
from jax import lax
from jax.experimental import pallas as pl
from jax.experimental.pallas import tpu as pltpu
from jax.sharding import PartitionSpec as P

AZIMUTH_COEF = 0.1
LANES = 128
SUB = 8


def tail_planes(rest):
    cuts = [0, rest // 2, rest]
    return [(a, b - a) for a, b in zip(cuts, cuts[1:]) if b > a]


def kernel(n_rad, n_az, n_local, source, offs, visc_in, absorb_in, result, depth,
           visc, absorb, heat, state, out, buf, sh, eo, ei, tot_out, tot_in, ss, rs, ls):
    groups = n_az // 2
    rad = lax.axis_index("rad")
    az = lax.axis_index("az")
    core = lax.rem(az, 2)
    sibling = {"az": az + 1 - 2 * core}
    planes, rows, width = state.shape
    cols = width // LANES
    tiles = rows // SUB
    dust = planes - 2
    rest = dust
    total_rows = rows * n_rad

    def rad_at(k):
        return {"rad": lax.rem(rad + k + n_rad, n_rad)}

    def az_at(k):
        return {"az": lax.rem(az + 2 * k, n_az)}

    count = [0]

    def remote(src, dst, device):
        i = count[0]
        count[0] += 1
        return pltpu.make_async_remote_copy(
            src_ref=src, dst_ref=dst, send_sem=ss.at[i], recv_sem=rs.at[i],
            device_id=device, device_id_type=pl.DeviceIdType.MESH,
        )

    fetch = pltpu.make_async_copy(source, state, ls.at[0])
    fetches = [fetch] + [
        pltpu.make_async_copy(a, b, ls.at[n_local + i])
        for i, (a, b) in enumerate(((visc_in, visc), (absorb_in, absorb)))
    ]
    stored = []

    def store(p0, np_, r0, nr):
        at = (pl.ds(p0, np_), pl.ds(r0, nr))
        c = pltpu.make_async_copy(out.at[at], result.at[at], ls.at[1 + len(stored)])
        c.start()
        stored.append(c)

    inner, outer = rad > 0, rad < n_rad - 1
    ei[...] = jnp.zeros_like(ei)
    tot_in[...] = jnp.zeros_like(tot_in)
    peers = [az_at(k) for k in range(1, groups)] + [sibling]
    barrier = pltpu.get_barrier_semaphore()
    for there, k in ((inner, -1), (outer, 1)):
        @pl.when(there)
        def _():
            pl.semaphore_signal(barrier, inc=1, device_id=rad_at(k), device_id_type=pl.DeviceIdType.MESH)
    for peer in peers:
        pl.semaphore_signal(barrier, inc=1, device_id=peer, device_id_type=pl.DeviceIdType.MESH)
    senders = len(peers)
    d = 1
    while d < n_rad:
        if d > 1:
            @pl.when(rad >= d)
            def _():
                pl.semaphore_signal(barrier, inc=1, device_id=rad_at(-d), device_id_type=pl.DeviceIdType.MESH)
            senders = senders + (rad + d < n_rad).astype(jnp.int32)
        d *= 2
    pl.semaphore_wait(barrier, senders + inner.astype(jnp.int32) + outer.astype(jnp.int32))

    pieces = [(dust, 2, 0, rows)]
    edge_tiles = [0, tiles - 1]
    for t in edge_tiles + list(range(1, tiles - 2)):
        pieces.append((0, rest, t * SUB, SUB))
    tail = tail_planes(rest)
    for p0, np_ in tail:
        pieces.append((p0, np_, (tiles - 2) * SUB, SUB))

    sent, chained = [], []
    across, beside = [], []
    for p0, np_, r0, nr in pieces:
        ps, rws = pl.ds(p0, np_), pl.ds(r0, nr)
        across.append([remote(source.at[ps, rws], buf.at[2 * k - 1, ps, rws], az_at(k)) for k in range(1, groups)])
        beside.append(remote(source.at[ps, rws], buf.at[0, ps, rws], sibling))
        for c in across[-1]:
            c.start()
            sent.append(c)
    for c in beside:
        c.start()
        sent.append(c)

    def arrive(i):
        p0, np_, r0, nr = pieces[i]
        ps, rws = pl.ds(p0, np_), pl.ds(r0, nr)
        forwards = []
        for k in range(1, groups):
            across[i][k - 1].wait_recv()
            f = remote(buf.at[2 * k - 1, ps, rws], buf.at[2 * k, ps, rws], sibling)
            f.start()
            sent.append(f)
            forwards.append(f)
        beside[i].wait_recv()
        for f in forwards:
            f.wait_recv()

    lane = lax.broadcasted_iota(jnp.int32, (SUB, LANES), 1)

    def shift_tile(tile, p0, np_):
        r = pl.ds(tile * SUB, SUB)
        sub = lax.broadcasted_iota(jnp.int32, (SUB, LANES), 0)
        amount = jnp.full((SUB, LANES), offs[tile * SUB], jnp.int32)
        for k in range(1, SUB):
            amount = jnp.where(sub == k, offs[tile * SUB + k], amount)
        block = amount // width
        within = amount - block * width
        column = within // LANES
        rem = within - column * LANES
        pick = (lane - rem) & (LANES - 1)
        low = lane < rem

        def one(p, carry):
            def load(d, c):
                cs = pl.ds(c * LANES, LANES)
                if d == 0:
                    return state[p, r, cs]
                if d % 2 == 0:
                    return buf[d - 1, p, r, cs]
                slot = jnp.where(core == 1, d, (d + 2) % n_az)
                return buf[slot - 1, p, r, cs]

            line = []
            for move, c in [(1, c) for c in range(cols)] + [(0, c) for c in range(cols)] + [(-1, 0)]:
                value = load(move % n_az, c)
                for b in range(1, n_az):
                    value = jnp.where(block == b, load((b + move) % n_az, c), value)
                line.append(value)
            step = cols // 2
            while step:
                chosen = (column & step) != 0
                line = [jnp.where(chosen, line[i - step], line[i]) for i in range(step, len(line))]
                step //= 2
            turned = [jnp.take_along_axis(v, pick, axis=1, mode="promise_in_bounds") for v in line]
            x = [turned[0]] + [jnp.where(low, turned[j - 1], turned[j]) for j in range(1, len(turned))]
            right = [pltpu.roll(v, 1, 1) for v in x[:-1]]
            left = [pltpu.roll(v, LANES - 1, 1) for v in x[1:]]
            for c in range(cols):
                cs = pl.ds(c * LANES, LANES)
                mid = x[c + 1]
                prev = jnp.where(lane == 0, right[c], right[c + 1])
                nxt = jnp.where(lane == LANES - 1, left[c + 1], left[c])
                sh[p, pl.ds(SUB + tile * SUB, SUB), cs] = mid
                out[p, r, cs] = mid + AZIMUTH_COEF * (nxt + prev - 2.0 * mid)
                if tile == 0:
                    eo[0, p, :, cs] = mid[:1]
                if tile == tiles - 1:
                    eo[1, p, :, cs] = mid[SUB - 1:]
            return carry

        lax.fori_loop(p0, p0 + np_, one, 0)

    hops = []

    def scan_send():
        i = len(hops)
        d = 1 << i
        if d < n_rad:
            c = remote(tot_out.at[i], tot_in.at[i], rad_at(d))
            goes = rad + d < n_rad
            pl.when(goes)(c.start)
            chained.append((goes, c))
            hops.append(c)

    def scan_take():
        i = len(hops) - 1
        pl.when(rad >= 1 << i)(hops[i].wait_recv)
        tot_out[i + 1] = tot_out[i] + tot_in[i]

    def send_edge(side, p0, np_):
        ps = pl.ds(p0, np_)
        c = remote(eo.at[side, ps], ei.at[1 - side, ps], rad_at(-1 if side == 0 else 1))
        goes, comes = (inner, outer) if side == 0 else (outer, inner)
        pl.when(goes)(c.start)
        chained.append((goes, c))
        return comes, c

    def edge_wait(edge):
        pl.when(edge[0])(edge[1].wait_recv)

    def place_edges(p0, np_):
        def one(p, carry):
            sh[p, SUB - 1:SUB, :] = jnp.where(rad > 0, ei[0, p], 0.0)
            sh[p, SUB + rows:SUB + rows + 1, :] = jnp.where(rad < n_rad - 1, ei[1, p], 0.0)
            return carry

        lax.fori_loop(p0, p0 + np_, one, 0)

    def smooth(tile, p0, np_):
        top = SUB + tile * SUB

        def one(p, carry):
            r = pl.ds(tile * SUB, SUB)
            mid = sh[p, top:top + SUB, :]
            up = sh[p, top - 1:top + SUB - 1, :]
            down = sh[p, top + 1:top + SUB + 1, :]
            out[p, r, :] = out[p, r, :] + visc[lax.rem(p, 2), r, :] * (down + up - 2.0 * mid)
            return carry

        lax.fori_loop(p0, p0 + np_, one, 0)

    for c in fetches:
        c.start()
    arrive(0)
    for c in fetches:
        c.wait()
    for t in range(tiles):
        shift_tile(t, dust, 2)
    edges = [send_edge(s, dust, 2) for s in (0, 1)]
    for e in edges:
        edge_wait(e)
    place_edges(dust, 2)
    for t in range(tiles):
        smooth(t, dust, 2)
    store(dust, 2, 0, rows)

    row = lax.broadcasted_iota(jnp.int32, (SUB, width), 0)
    for h in range(2):
        base = jnp.zeros((1, width), jnp.float32)
        for t in range(tiles):
            r = pl.ds(t * SUB, SUB)
            step = 2.0 * absorb[h, r, :] * out[dust + h, r, :] / total_rows
            run = step
            for k in (1, 2, 4):
                run = run + jnp.where(row >= k, pltpu.roll(run, k, 0), 0.0)
            run = run + base
            depth[h, r, :] = run - 0.5 * step
            base = run[SUB - 1:]
        tot_out[0, h] = base
    scan_send()
    arrive(1)
    shift_tile(0, 0, rest)
    edge_in = send_edge(0, 0, rest)
    scan_take()
    scan_send()
    arrive(2)
    shift_tile(tiles - 1, 0, rest)
    edge_out = send_edge(1, 0, rest)

    scan_take()
    while 1 << len(hops) < n_rad:
        scan_send()
        scan_take()
    for h in range(2):
        carried = tot_in[0, h]
        for i in range(1, len(hops)):
            carried = carried + tot_in[i, h]
        for t in range(tiles):
            r = pl.ds(t * SUB, SUB)
            radius = (rad * rows + t * SUB + row).astype(jnp.float32) + 0.5
            flux = 1.0 / (1.0 + radius / total_rows)
            depth[h, r, :] = depth[h, r, :] + carried
            heat[h, r, :] = flux * jnp.exp(-depth[h, r, :])

    def warm(tile):
        r = pl.ds(tile * SUB, SUB)
        for h in range(2):
            out[rest - 2 + h, r, :] = out[rest - 2 + h, r, :] + heat[h, r, :]

    edge_wait(edge_in)
    edge_wait(edge_out)
    place_edges(0, rest)
    i = 3
    for t in range(1, tiles - 2):
        arrive(i)
        shift_tile(t, 0, rest)
        smooth(t - 1, 0, rest)
        warm(t - 1)
        store(0, rest, (t - 1) * SUB, SUB)
        i += 1
    first = max(tiles - 3, 0)
    for p0, np_ in tail:
        arrive(i)
        shift_tile(tiles - 2, p0, np_)
        for t in range(first, tiles):
            smooth(t, p0, np_)
            if p0 + np_ == rest:
                warm(t)
        store(p0, np_, first * SUB, (tiles - first) * SUB)
        i += 1
    for c in stored:
        c.wait()
    for goes, c in chained:
        pl.when(goes)(c.wait_send)
    for c in sent:
        c.wait_send()


def body(n_rad, n_az, state, offsets, viscosity, absorb):
    fields, polar, rows, width = state.shape
    planes = fields * polar
    groups = n_az // 2
    tiles = rows // SUB
    n_tail = len(tail_planes(planes - 2))
    n_pieces = 1 + 2 + max(tiles - 3, 0) + n_tail
    n_scan = (n_rad - 1).bit_length()
    n_local = 2 + max(tiles - 3, 0) + n_tail
    n_sems = n_pieces * (2 * (groups - 1) + 1) + 4 + n_scan
    f32 = jnp.float32
    vm = pl.BlockSpec(memory_space=pltpu.VMEM)
    hbm = pl.BlockSpec(memory_space=pl.ANY)
    moved, local = pl.pallas_call(
        functools.partial(kernel, n_rad, n_az, n_local),
        out_shape=(
            jax.ShapeDtypeStruct((planes, rows, width), f32),
            jax.ShapeDtypeStruct((polar, rows, width), f32),
        ),
        in_specs=[hbm, pl.BlockSpec(memory_space=pltpu.SMEM), hbm, hbm],
        out_specs=(hbm, vm),
        scratch_shapes=[
            pltpu.VMEM((polar, rows, width), f32),
            pltpu.VMEM((polar, rows, width), f32),
            pltpu.VMEM((polar, rows, width), f32),
            pltpu.VMEM((planes, rows, width), f32),
            pltpu.VMEM((planes, rows, width), f32),
            pltpu.VMEM((n_az - 1, planes, rows, width), f32),
            pltpu.VMEM((planes, rows + 2 * SUB, width), f32),
            pltpu.VMEM((2, planes, 1, width), f32),
            pltpu.VMEM((2, planes, 1, width), f32),
            pltpu.VMEM((n_scan + 1, polar, 1, width), f32),
            pltpu.VMEM((n_scan, polar, 1, width), f32),
            pltpu.SemaphoreType.DMA((n_sems,)),
            pltpu.SemaphoreType.DMA((n_sems,)),
            pltpu.SemaphoreType.DMA((n_local + 2,)),
        ],
        compiler_params=pltpu.CompilerParams(
            collective_id=0, has_side_effects=True, vmem_limit_bytes=56 * 2**20
        ),
    )(state.reshape(planes, rows, width), offsets, viscosity, absorb)
    moved = moved.reshape(state.shape)
    return moved, local


def solution(mesh):
    in_specs = (P(None, None, "rad", "az"), P("rad"), P(None, "rad", "az"), P(None, "rad", "az"))
    out_specs = (P(None, None, "rad", "az"), P(None, "rad", "az"))
    f = functools.partial(body, mesh.shape["rad"], mesh.shape["az"])
    return jax.shard_map(f, mesh=mesh, in_specs=in_specs, out_specs=out_specs, check_vma=False)
```
